32 devices in a mesh: group: 2 (over x), shard: 16 (over z, y, core).
Axes of the slice: x: 2, y: 2, z: 4, core: 2. Of those that a mesh axis runs over, the one named last changes fastest.
Arguments:
- tokens: bfloat16 [128, 3072], P('group', 'shard'), may hold values from -6 to 6
- cotangent: bfloat16 [128, 3072], P('group', 'shard'), may hold values from -1.5 to 1.5
- expert_ids: int32 [128, 2], P('group'), may hold values from 0 to 7, all different within a row; in each aligned block of 64 rows (0 to 63, 64 to 127, ...) at most 36 rows name the same one
- route_weight: float32 [128, 2], P('group'), may hold values from 0.1 to 0.9
- w_gate: bfloat16 [8, 3072, 8192], P('group', None, 'shard'), may hold values from -0.109375 to 0.109375
- w_up: bfloat16 [8, 3072, 8192], P('group', None, 'shard'), may hold values from -0.109375 to 0.109375
- w_down: bfloat16 [8, 8192, 3072], P('group', 'shard'), may hold values from -0.109375 to 0.109375
Outputs:
- grad_tokens: bfloat16 [128, 3072], P('group', 'shard')
- grad_gate: bfloat16 [8, 3072, 8192], P('group', None, 'shard')
- grad_up: bfloat16 [8, 3072, 8192], P('group', None, 'shard')
The draws below stay inside these ranges and needn't reach their ends.
Inputs may be any that keep to these rules, and one draw needn't show every extreme that they name: `expert_ids`: each token names 2 different experts. Among the 64 tokens of one aligned block (the tokens of one index of group), no expert is named by more than 36 tokens.
All inputs are finite; a program needn't handle non-finite values.
Results may differ from the reference program's by a relative error of at most 0.0064.
Values may be sent and summed in bfloat16 or wider, within the bound.
No kernel may reach another device: no remote copies, remote signals or barrier semaphores. Data moves between devices by JAX's collectives and lax.ppermute only.
A program may use at most 192 MiB of HBM per device.

```python
import math
import jax
import jax.numpy as jnp
import numpy as np
from jax import lax

D = 3072
FF = 8192
EXPERTS = 8
TOPK = 2
TOK_GRP = 64
CAP = 36
TOKENS = 128
N_GROUP = 2


def block_scale(stream_key, extent, split, low, largest):
    factor_of, own = 1.0, jax.random.fold_in(stream_key, 6)
    for position, parts in split:
        heights = jnp.exp(jax.random.uniform(jax.random.fold_in(own, position), (parts,), jnp.float32, low / len(split), largest / len(split)))
        factor_of = factor_of * jnp.repeat(heights, extent[position] // parts).reshape([-1 if axis == position else 1 for axis in range(len(extent))])
    return factor_of


def routed_block(rng, own, number, rows, number_of, top, limit, skew):
    order = jax.random.permutation(rng, number_of)
    crowded, common = shares(number_of, rows * top, limit, skew, True), shares(number_of, rows * top, limit, skew, False)
    places = jnp.arange(number_of)

    def named(lengths, turn):
        used = int((lengths > 0).sum())
        fixed = max(1, used // 4)
        passed = fixed + (places - fixed + turn * (used - fixed)) % max(1, number_of - fixed)
        return jnp.zeros((number_of,), jnp.int32).at[order[jnp.where(places < fixed, places, passed)]].set(jnp.asarray(lengths, jnp.int32))

    lengths = jnp.where(number % 4 == 0, named(crowded, number // 4), named(common, number - number // 4 - 1))
    mixed = jax.random.permutation(jax.random.fold_in(own, 3), number_of)
    donor, taker = mixed[0:number_of // 2 * 2:2], mixed[1:number_of // 2 * 2:2]
    margin = jnp.minimum(lengths[donor] - 1, limit - lengths[taker]) // 2
    margin = jnp.where((donor == order[0]) | (taker == order[0]) | (lengths[taker] == 0), 0, jnp.maximum(margin, 0))
    passed = jax.random.randint(jax.random.fold_in(own, 4), (number_of // 2,), 0, 1 << 20) % (margin + 1)
    lengths = lengths.at[donor].add(-passed).at[taker].add(passed)
    members = jnp.searchsorted(jnp.cumsum(lengths), jnp.arange(rows * top), side="right").astype(jnp.int32)
    listing = members.reshape(top, rows).T
    listing = listing[jax.random.permutation(jax.random.fold_in(own, 1), rows)]
    turn = jax.random.randint(jax.random.fold_in(own, 2), (rows, 1), 0, top)
    return jnp.take_along_axis(listing, (jnp.arange(top)[None, :] + turn) % top, axis=1)


def shares(number_of, total, bound, lean, full):
    loads = [(1 << 20) // math.isqrt(rank ** lean) + 1 for rank in range(1, number_of + 1)]
    largest = bound if full else min(bound, max(-(-total // number_of), total * loads[0] // sum(loads)))
    least = 1 if total - largest >= number_of - 1 else 0
    counts, rest = [largest] + [least] * (number_of - 1), total - largest - least * (number_of - 1)
    while rest > 0:
        movable = [i for i in range(1, number_of) if counts[i] < largest] or [i for i in range(1, number_of) if counts[i] < bound]
        pool, remaining = sum([loads[i] for i in movable]), rest
        for i in movable:
            more = min(bound - counts[i], max(1, remaining * loads[i] // pool), rest)
            counts[i] = counts[i] + more
            rest = rest - more
    return np.array(counts)


def bell_draw(own_key, shape, width, limit, pieces=(), kind=jnp.bfloat16):
    entries = jax.random.normal(own_key, shape, jnp.float32) * width
    if len(pieces) > 0:
        entries = block_scale(own_key, shape, pieces, -0.22, 0.18) * entries
    return jnp.clip(entries, min=-limit, max=limit).astype(kind)


def setup_inputs(seed: int = 0) -> dict:
    key_list = jax.random.split(jax.random.key(seed), 8)
    tokens = bell_draw(key_list[0], (TOKENS, D), 1.0, 6.0, ((0, 2), (1, 16)))
    cotangent = bell_draw(key_list[1], (TOKENS, D), 0.25, 1.5, ((0, 2), (1, 16)))
    expert_ids_keys = jax.random.split(jax.random.fold_in(key_list[2], 1), TOKENS // TOK_GRP)
    expert_ids_turns = jax.random.permutation(jax.random.fold_in(key_list[2], 3), TOKENS // TOK_GRP)
    expert_ids = jax.vmap(lambda own, number: routed_block(jax.random.fold_in(key_list[2], 2), own, number, TOK_GRP, EXPERTS, TOPK, CAP, 2))(expert_ids_keys, expert_ids_turns).reshape((TOKENS, TOPK))
    route_weight = jnp.clip(0.1 + 0.79999997 * jax.random.uniform(key_list[3], (TOKENS, TOPK), jnp.float32) ** block_scale(key_list[3], (TOKENS, TOPK), ((0, 2),), -0.2, 0.2), 0.1, 0.9)
    w_gate = bell_draw(key_list[4], (EXPERTS, D, FF), D ** -0.5, 0.109375, ((0, 2), (2, 16)))
    w_up = bell_draw(key_list[5], (EXPERTS, D, FF), D ** -0.5, 0.109375, ((0, 2), (2, 16)))
    w_down = bell_draw(key_list[6], (EXPERTS, FF, D), D ** -0.5, 0.109375, ((0, 2), (1, 16)))
    return dict(tokens=tokens, cotangent=cotangent, expert_ids=expert_ids, route_weight=route_weight, w_gate=w_gate, w_up=w_up, w_down=w_down)


exact_mode = lax.Precision.HIGHEST


def slot_table(expert_ids, capacity):
    experts_axis = jnp.arange(EXPERTS, dtype=jnp.int32)
    counted = jnp.sum((expert_ids[:, :, None] == experts_axis[None, None, :]).astype(jnp.int32), axis=1)
    ranking = jnp.cumsum(counted, axis=0).astype(jnp.int32) - 1
    places = jnp.arange(capacity, dtype=jnp.int32)
    slot_map = (counted.T[:, None, :] == 1) & (ranking.T[:, None, :] == places[None, :, None])
    return counted, slot_map


def slot_scales(slot_map, expert_ids, route_weight):
    experts_axis = jnp.arange(EXPERTS, dtype=jnp.int32)
    per_expert = jnp.sum(jnp.where(expert_ids[:, :, None] == experts_axis[None, None, :], route_weight[:, :, None], jnp.float32(0.0)), axis=1)
    return jnp.einsum("ect,te->ec", slot_map.astype(jnp.float32), per_expert, precision=exact_mode)


def slot_grads(slot_inputs, slot_cotangents, paired, down_weight):
    hidden_width = down_weight.shape[0]
    joined = jnp.dot(slot_inputs, paired, preferred_element_type=jnp.float32)
    gate_pre = joined[:, :hidden_width]
    up_value = joined[:, hidden_width:]
    sigmoid_gate = jax.nn.sigmoid(gate_pre)
    active = gate_pre * sigmoid_gate
    hidden_grad = lax.dot_general(slot_cotangents, down_weight, (((1,), (1,)), ((), ())), preferred_element_type=jnp.float32)
    gate_grad = (hidden_grad * up_value * sigmoid_gate * (1.0 + gate_pre * (1.0 - sigmoid_gate))).astype(jnp.bfloat16)
    up_grad = (hidden_grad * active).astype(jnp.bfloat16)
    stacked = jnp.concatenate([gate_grad, up_grad], axis=1)
    input_grad = lax.dot_general(stacked, paired, (((1,), (1,)), ((), ())), preferred_element_type=jnp.float32)
    return input_grad, stacked


def source_partials(slot_inputs, stacked, sources):
    capacity = slot_inputs.shape[0] // sources

    def accumulate(source, running):
        begin = (source * capacity).astype(jnp.int32)
        piece_inputs = lax.dynamic_slice_in_dim(slot_inputs, begin, capacity, 0)
        piece_grads = lax.dynamic_slice_in_dim(stacked, begin, capacity, 0)
        partial_sum = lax.dot_general(piece_inputs, piece_grads, (((0,), (0,)), ((), ())), preferred_element_type=jnp.float32)
        return running + lax.optimization_barrier(partial_sum.astype(jnp.bfloat16)).astype(jnp.float32)

    initial = jnp.zeros((slot_inputs.shape[1], stacked.shape[1]), jnp.float32)
    return lax.fori_loop(jnp.int32(0), jnp.int32(sources), accumulate, initial)


def reference(tokens, cotangent, expert_ids, route_weight, w_gate, w_up, w_down):
    by_group = tokens.reshape(N_GROUP, TOK_GRP, D).astype(jnp.float32)
    cot_group = cotangent.reshape(N_GROUP, TOK_GRP, D).astype(jnp.float32)
    ids_group = expert_ids.reshape(N_GROUP, TOK_GRP, TOPK)
    weights_group = route_weight.reshape(N_GROUP, TOK_GRP, TOPK)
    tables = []
    scale_list = []
    for group_id in range(N_GROUP):
        counted, slot_map = slot_table(ids_group[group_id], CAP)
        tables.append(slot_map)
        scale_list.append(slot_scales(slot_map, ids_group[group_id], weights_group[group_id]))
    table_all = jnp.stack(tables)
    scale_all = jnp.stack(scale_list)
    grad_total = jnp.zeros((N_GROUP, TOK_GRP, D), jnp.float32)
    gate_grads = []
    up_grads = []
    for expert in range(EXPERTS):
        chosen = table_all[:, expert].astype(jnp.float32)
        slot_inputs = jnp.einsum("gct,gtd->gcd", chosen, by_group, precision=exact_mode).astype(jnp.bfloat16).reshape(N_GROUP * CAP, D)
        picked = jnp.einsum("gct,gtd->gcd", chosen, cot_group, precision=exact_mode)
        slot_cotangents = (scale_all[:, expert][:, :, None] * picked).astype(jnp.bfloat16).reshape(N_GROUP * CAP, D)
        paired = jnp.concatenate([w_gate[expert], w_up[expert]], axis=1)
        input_grad, stacked = slot_grads(slot_inputs, slot_cotangents, paired, w_down[expert])
        grad_total = grad_total + jnp.einsum("gct,gcd->gtd", chosen, input_grad.reshape(N_GROUP, CAP, D), precision=exact_mode)
        running = source_partials(slot_inputs, stacked, N_GROUP)
        gate_grads.append(running[:, :FF].astype(jnp.bfloat16))
        up_grads.append(running[:, FF:].astype(jnp.bfloat16))
    return grad_total.reshape(TOKENS, D).astype(jnp.bfloat16), jnp.stack(gate_grads), jnp.stack(up_grads)
```

```python
import jax
import jax.numpy as jnp
from jax import lax
from jax.experimental import pallas as pl
from jax.experimental.pallas import tpu as pltpu
from jax.sharding import PartitionSpec as P

BF = jnp.bfloat16
F32 = jnp.float32
BOTH = ("group", "shard")
MIB = 1 << 20
VM = pl.BlockSpec(memory_space=pltpu.VMEM)
SM = pl.BlockSpec(memory_space=pltpu.SMEM)


def dot(a, b, da, db):
    return lax.dot_general(a, b, (((da,), (db,)), ((), ())), preferred_element_type=F32)


def bits_of(size):
    return size.bit_length() - 1


def stage_masks(groups, shards):
    masks = [1 << k for k in range(bits_of(shards) - 1, 0, -1)] + [shards << k for k in range(bits_of(groups))]
    other = masks[:-2] + masks[-2:][::-1]
    return other, masks


def swap(x, groups, shards, masks):
    pairs = [(i, i ^ masks[i & 1]) for i in range(groups * shards)]
    return lax.ppermute(x, BOTH, pairs)


def relative(index, masks, top_first):
    count = len(masks)
    out = 0
    for step, mask in enumerate(masks):
        place = count - 1 - step if top_first else step
        out = out | (((index >> bits_of(mask)) & 1) << place)
    return out


def forward_kernel(gather_masks, scatter_masks, groups, shards, experts,
                   place, own0, own1, oth0, oth1, routes, wg, wu, wd,
                   full, grads, keep, send, x, q, coef, total):
    half = own0.shape[0]
    rows, width = own0.shape[1], own0.shape[2]
    tokens = groups * rows
    hidden = wg.shape[2]
    core = place[0]
    group = place[1]

    def assemble(out, low, high, masks, start):
        for g in range(groups):
            for pair in range(shards // 2):
                r = relative(g * shards + pair * 2, masks, False) ^ start
                into = (pl.ds(g * rows, rows), pl.ds(pair * width, width))

                @pl.when(r < half)
                def _():
                    out[into] = low[jnp.minimum(r, half - 1)]

                @pl.when(r >= half)
                def _():
                    out[into] = high[jnp.maximum(r - half, 0)]

    @pl.when(core == 0)
    def _():
        assemble(x, own0, own1, gather_masks[0], place[2])
        assemble(q, oth0, oth1, gather_masks[1], place[3])

    @pl.when(core == 1)
    def _():
        assemble(x, oth0, oth1, gather_masks[0], place[2])
        assemble(q, own0, own1, gather_masks[1], place[3])

    full[...] = x[...]
    for g in range(groups):
        table = routes[g ^ group].T
        for e in range(experts):
            number = (group * experts + e).astype(F32)
            value = jnp.where(table[:, 0:1] == number, table[:, 2:3], 0.0) + jnp.where(table[:, 1:2] == number, table[:, 3:4], 0.0)
            coef[e, g * rows:(g + 1) * rows, :] = value

    @pl.loop(0, experts)
    def _(e):
        gate_pre = dot(x[...], wg[e], 1, 0)
        up_value = dot(x[...], wu[e], 1, 0)
        hidden_grad = dot(q[...], wd[e], 1, 1) * coef[e]
        s = 1.0 / (1.0 + jnp.exp(-gate_pre))
        gate_grad = (hidden_grad * up_value * s * (1.0 + gate_pre * (1.0 - s))).astype(BF)
        up_grad = (hidden_grad * (gate_pre * s)).astype(BF)
        grads[e, :, :hidden] = gate_grad
        grads[e, :, hidden:] = up_grad
        part = dot(gate_grad, wg[e], 1, 1) + dot(up_grad, wu[e], 1, 1)

        @pl.when(e == 0)
        def _():
            total[...] = part

        @pl.when(e > 0)
        def _():
            total[...] += part

    part_rows = rows // 2
    for g in range(groups):
        for pair in range(shards // 2):
            at = g * shards + pair * 2
            first = relative(at, scatter_masks[0], True) ^ place[4]
            second = relative(at, scatter_masks[1], True) ^ place[5]
            columns = pl.ds(pair * width, width)
            upper = total[g * rows:g * rows + part_rows, columns]
            lower = total[g * rows + part_rows:(g + 1) * rows, columns]

            @pl.when(core == 0)
            def _():
                keep[first] = upper
                send[second] = lower

            @pl.when(core == 1)
            def _():
                keep[second] = lower
                send[first] = upper


def weight_kernel(xt, grads, *rest):
    out_gate, out_up = rest[-2:]
    hidden = out_gate.shape[2]
    block = out_gate.shape[1]
    rows = xt[pl.ds(pl.program_id(0) * block, block), :]
    out_gate[0] = dot(rows, grads[0, :, :hidden], 1, 0).astype(BF)
    out_up[0] = dot(rows, grads[0, :, hidden:], 1, 0).astype(BF)


def weight_grads(xt, grads, expert, so_far, shape):
    features, tokens = xt.shape
    steps = 2
    block = features // steps
    out = jax.ShapeDtypeStruct(shape, BF)
    out_spec = pl.BlockSpec((1, block, shape[2]), lambda j: (expert, j, 0))
    aliases = {2: 0, 3: 1} if so_far else {}
    return pl.pallas_call(
        weight_kernel,
        grid=(steps,),
        out_shape=(out, out),
        in_specs=[
            pl.BlockSpec((features, tokens), lambda j: (0, 0)),
            pl.BlockSpec((1,) + grads.shape[1:], lambda j: (expert, 0, 0)),
        ] + [pl.BlockSpec(memory_space=pl.ANY)] * len(so_far),
        out_specs=(out_spec, out_spec),
        input_output_aliases=aliases,
        compiler_params=pltpu.CompilerParams(vmem_limit_bytes=24 * MIB),
        cost_estimate=pl.CostEstimate(flops=4 * features * tokens * shape[2], bytes_accessed=4 * features * shape[2], transcendentals=0),
        name="weight_grads",
    )(xt, grads, *so_far)


def body(tokens, cotangent, expert_ids, route_weight, w_gate, w_up, w_down):
    groups, shards = lax.axis_size("group"), lax.axis_size("shard")
    group, shard = lax.axis_index("group"), lax.axis_index("shard")
    experts, features, hidden = w_gate.shape
    rows, width = tokens.shape
    core = shard & 1
    me = group * shards + shard
    gather_masks = stage_masks(groups, shards)
    scatter_masks = tuple(m[::-1] for m in gather_masks)
    first = core == 0
    mine, theirs = jnp.where(first, tokens, cotangent), jnp.where(first, cotangent, tokens)
    got = swap(theirs, groups, shards, (1, 1))
    block = jnp.where(first, jnp.concatenate([mine, got], 1), jnp.concatenate([got, mine], 1))[None]
    routes = jnp.concatenate([expert_ids.astype(F32).T, route_weight.T, jnp.zeros((4, rows), F32)], 0)[None]
    for k in range(bits_of(groups)):
        routes = jnp.concatenate([routes, swap(routes, groups, shards, (shards << k,) * 2)], 0)
    count = len(gather_masks[0])
    for step in range(count - 1):
        block = jnp.concatenate([block, swap(block, groups, shards, (gather_masks[0][step], gather_masks[1][step]))], 0)
    low = block
    high = swap(low, groups, shards, (gather_masks[0][-1], gather_masks[1][-1]))
    other_low = swap(low, groups, shards, (1, 1))
    other_high = swap(high, groups, shards, (1, 1))
    place = jnp.stack([core, group, relative(me, gather_masks[0], False), relative(me, gather_masks[1], False),
                       relative(me, scatter_masks[0], True), relative(me, scatter_masks[1], True)]).astype(jnp.int32)
    pairs = groups * shards // 2
    total_rows = groups * rows
    in_vmem = [pltpu.with_memory_space_constraint(w, pltpu.VMEM) for w in (w_gate, w_up, w_down)]
    piece = jax.ShapeDtypeStruct((pairs, rows // 2, 2 * width), F32)

    def forward(*refs):
        forward_kernel(gather_masks, scatter_masks, groups, shards, experts, *refs)

    full, grads, keep, send = pl.pallas_call(
        forward,
        out_shape=(jax.ShapeDtypeStruct((total_rows, features), BF), jax.ShapeDtypeStruct((experts, total_rows, 2 * hidden), BF), piece, piece),
        in_specs=[SM] + [VM] * 8,
        out_specs=(VM,) * 4,
        scratch_shapes=[pltpu.VMEM((total_rows, features), BF), pltpu.VMEM((total_rows, features), BF),
                        pltpu.VMEM((experts, total_rows, 1), F32), pltpu.VMEM((total_rows, features), F32)],
        compiler_params=pltpu.CompilerParams(vmem_limit_bytes=20 * MIB),
        name="forward",
    )(place, low, high, other_low, other_high, routes, *in_vmem)

    xt = full.T
    so_far = ()
    for e in range(experts):
        so_far = weight_grads(xt, grads, e, so_far, w_gate.shape)

    kept = keep + swap(send, groups, shards, (1, 1))
    for step in range(count):
        half = kept.shape[0] // 2
        sent = kept[half:]
        if 2 * step < count:
            sent = sent.astype(BF)
        kept = kept[:half] + swap(sent, groups, shards, (scatter_masks[0][step], scatter_masks[1][step])).astype(F32)
    done = kept[0].astype(BF)
    left, right = done[:, :width], done[:, width:]
    got = swap(jnp.where(first, right, left), groups, shards, (1, 1))
    stay = jnp.where(first, left, right)
    grad_tokens = jnp.where(first, jnp.concatenate([stay, got], 0), jnp.concatenate([got, stay], 0))
    return grad_tokens, so_far[0], so_far[1]


def solution(mesh):
    in_specs = (
        P("group", "shard"),
        P("group", "shard"),
        P("group", None),
        P("group", None),
        P("group", None, "shard"),
        P("group", None, "shard"),
        P("group", "shard", None),
    )
    out_specs = (P("group", "shard"), P("group", None, "shard"), P("group", None, "shard"))
    return jax.shard_map(body, mesh=mesh, in_specs=in_specs, out_specs=out_specs, check_vma=False)
```

```python
import jax
import jax.numpy as jnp
from jax import lax
from jax.experimental import pallas as pl
from jax.experimental.pallas import tpu as pltpu
from jax.sharding import PartitionSpec as P

BF = jnp.bfloat16
F32 = jnp.float32
BOTH = ("group", "shard")
MIB = 1 << 20
VM = pl.BlockSpec(memory_space=pltpu.VMEM)
SM = pl.BlockSpec(memory_space=pltpu.SMEM)


def dot(a, b, da, db):
    return lax.dot_general(a, b, (((da,), (db,)), ((), ())), preferred_element_type=F32)


def bits_of(size):
    return size.bit_length() - 1


def stage_masks(groups, shards):
    masks = [1 << k for k in range(bits_of(shards) - 1, 0, -1)] + [shards << k for k in range(bits_of(groups))]
    other = masks[:-2] + masks[-2:][::-1]
    return other, masks


def swap(x, groups, shards, masks):
    pairs = [(i, i ^ masks[i & 1]) for i in range(groups * shards)]
    return lax.ppermute(x, BOTH, pairs)


def relative(index, masks, top_first):
    count = len(masks)
    out = 0
    for step, mask in enumerate(masks):
        place = count - 1 - step if top_first else step
        out = out | (((index >> bits_of(mask)) & 1) << place)
    return out


def forward_kernel(gather_masks, scatter_masks, groups, shards, experts,
                   t0, t1, t2, t3, c0, c1, c2, c3, routes, wg_hbm, wu_hbm, wd_hbm,
                   full, grads, keep, send, x, q, coef, total, wg, wu, wd, sems):
    half, rows, width = t0.shape[0], t0.shape[1], t0.shape[2] // 2
    tokens = 2 * groups * rows
    hidden = wg.shape[2]
    group, shard = lax.axis_index("group"), lax.axis_index("shard")
    core, me = shard & 1, group * shards + shard
    gather_at = [relative(me, masks, False) for masks in gather_masks]
    scatter_at = [relative(me, masks, True) for masks in scatter_masks]

    def fetch(i, e):
        source, target = ((wg_hbm, wg), (wu_hbm, wu), (wd_hbm, wd))[i]
        return pltpu.make_async_copy(source.at[e], target.at[e], sems.at[i, e])

    for e in range(experts):
        for i in range(3):
            fetch(i, e).start()

    def assemble(out, even, odd):
        for g in range(groups):
            for pair in range(shards // 2):
                at = g * shards + pair * 2
                blocks = []
                for (low, high), masks, start in ((even, gather_masks[0], gather_at[0]), (odd, gather_masks[1], gather_at[1])):
                    r = relative(at, masks, False) ^ start
                    blocks.append(jnp.where(r < half, low[jnp.minimum(r, half - 1)], high[jnp.maximum(r - half, 0)]))
                for k in range(2):
                    out[(2 * g + k) * rows:(2 * g + k + 1) * rows, pair * 2 * width:(pair + 1) * 2 * width] = jnp.concatenate(
                        [block[:, k * width:(k + 1) * width] for block in blocks], axis=1)

    @pl.when(core == 0)
    def _():
        assemble(x, (t0, t1), (t2, t3))
        assemble(q, (c0, c1), (c2, c3))

    @pl.when(core == 1)
    def _():
        assemble(x, (t2, t3), (t0, t1))
        assemble(q, (c2, c3), (c0, c1))

    full[...] = x[...]
    for g in range(groups):
        table = routes[g ^ group].T
        for e in range(experts):
            number = (group * experts + e).astype(F32)
            value = jnp.where(table[:, 0:1] == number, table[:, 2:3], 0.0) + jnp.where(table[:, 1:2] == number, table[:, 3:4], 0.0)
            coef[e, 2 * g * rows:2 * (g + 1) * rows, :] = value

    @pl.loop(0, experts)
    def _(e):
        fetch(0, e).wait()
        gate_pre = dot(x[...], wg[e], 1, 0)
        fetch(1, e).wait()
        up_value = dot(x[...], wu[e], 1, 0)
        fetch(2, e).wait()
        hidden_grad = dot(q[...], wd[e], 1, 1) * coef[e]
        s = 1.0 / (1.0 + jnp.exp(-gate_pre))
        gate_grad = (hidden_grad * up_value * s * (1.0 + gate_pre * (1.0 - s))).astype(BF)
        up_grad = (hidden_grad * (gate_pre * s)).astype(BF)
        grads[e, :, :hidden] = gate_grad
        grads[e, :, hidden:] = up_grad
        part = dot(gate_grad, wg[e], 1, 1) + dot(up_grad, wu[e], 1, 1)

        @pl.when(e == 0)
        def _():
            total[...] = part

        @pl.when(e > 0)
        def _():
            total[...] += part

    for g in range(groups):
        for pair in range(shards // 2):
            at = g * shards + pair * 2
            first = relative(at, scatter_masks[0], True) ^ scatter_at[0]
            second = relative(at, scatter_masks[1], True) ^ scatter_at[1]
            block = total[2 * g * rows:2 * (g + 1) * rows, pair * 2 * width:(pair + 1) * 2 * width]
            even, odd = (jnp.concatenate([block[:rows, k * width:(k + 1) * width], block[rows:, k * width:(k + 1) * width]], axis=1) for k in range(2))

            @pl.when(core == 0)
            def _():
                keep[first] = even
                send[second] = odd.astype(BF)

            @pl.when(core == 1)
            def _():
                keep[second] = odd
                send[first] = even.astype(BF)


def pack_kernel(tokens, cotangent, ids, weights, packed, routes):
    half = tokens.shape[0] // 2
    for i, a in enumerate((tokens, cotangent)):
        packed[i, 0] = jnp.concatenate([a[:half, :], a[half:, :]], axis=1)
    routes[0] = jnp.zeros_like(routes[0])
    routes[0, 0:2, :] = ids[...].astype(F32)
    routes[0, 2:4, :] = weights[...]


def pack(tokens, cotangent, ids, weights):
    rows, width = tokens.shape
    return pl.pallas_call(
        pack_kernel,
        out_shape=(pltpu.VMEM((2, 1, rows // 2, 2 * width), BF), pltpu.VMEM((1, 8, rows), F32)),
        in_specs=[VM] * 4,
        out_specs=(VM, VM),
        name="pack",
    )(tokens, cotangent, ids.T, weights.T)


def weight_kernel(units, blocks, transposed, *refs):
    rows, grads = refs[0], refs[1]
    if transposed:
        out_gate, out_up, token, made, sems = refs[-5:]
        xt = rows
    else:
        out_gate, out_up, token, xt, made, sems = refs[-6:]
        xt[...] = rows[...].T
    features, hidden = xt.shape[0], out_gate.shape[2]
    block = features // blocks
    copies = []
    for k, unit in enumerate(units):
        expert, j = divmod(unit, blocks)
        at = slice(j * block, (j + 1) * block)
        for i, out in enumerate((out_gate, out_up)):
            made[i, k] = dot(xt[at, :], grads[expert, :, i * hidden:(i + 1) * hidden], 1, 0).astype(BF)
            copies.append(pltpu.make_async_copy(made.at[i, k], out.at[expert, at, :], sems.at[i, k]))
            copies[-1].start()
    token[...] = jnp.zeros_like(token)
    for copy in copies:
        copy.wait()


def weight_grads(rows, grads, after, so_far, units, blocks, shape, piece):
    experts, features, hidden = shape
    transposed = bool(so_far)
    array, zero = jax.ShapeDtypeStruct(shape, BF), pltpu.VMEM((1,) + piece[1:], F32)
    anywhere = pl.BlockSpec(memory_space=pl.ANY)

    def kernel(*refs):
        weight_kernel(units, blocks, transposed, *refs)

    return pl.pallas_call(
        kernel,
        out_shape=(array, array, zero) + (() if transposed else (pltpu.VMEM((features, rows.shape[0]), BF),)),
        in_specs=[VM, VM, anywhere] + [anywhere] * len(so_far),
        out_specs=(anywhere, anywhere, VM) + (() if transposed else (VM,)),
        input_output_aliases={3: 0, 4: 1} if transposed else {},
        scratch_shapes=[pltpu.VMEM((2, len(units), features // blocks, hidden), BF), pltpu.SemaphoreType.DMA((2, len(units)))],
        compiler_params=pltpu.CompilerParams(vmem_limit_bytes=16 * MIB),
        cost_estimate=pl.CostEstimate(flops=4 * features * grads.shape[1] * hidden, bytes_accessed=4 * features * hidden, transcendentals=0),
        name="weight_grads",
    )(*(pltpu.with_memory_space_constraint(a, pltpu.VMEM) for a in (rows, grads)), after, *so_far)


def body(tokens, cotangent, expert_ids, route_weight, w_gate, w_up, w_down):
    groups, shards = lax.axis_size("group"), lax.axis_size("shard")
    experts, features, hidden = w_gate.shape
    rows, width = tokens.shape
    half_rows = rows // 2
    gather_masks = stage_masks(groups, shards)
    scatter_masks = tuple(m[::-1] for m in gather_masks)
    count = len(gather_masks[0])
    pairs = groups * shards // 2

    def step_masks(masks, step):
        return masks[0][step], masks[1][step]

    packed, routes = pack(tokens, cotangent, expert_ids, route_weight)
    def exchange(r):
        for k in range(bits_of(groups)):
            r = jnp.concatenate([r, swap(r, groups, shards, (shards << k,) * 2)], 0)
        return r

    routes = exchange(routes)
    for step in range(count - 2):
        packed = jnp.concatenate([packed, swap(packed, groups, shards, step_masks(gather_masks, step))], 1)
    packed, routes = lax.optimization_barrier((packed, routes))
    chains = [packed[0], packed[1]]
    chains = [jnp.concatenate([a, swap(a, groups, shards, step_masks(gather_masks, count - 2))], 0) for a in chains]
    highs = [swap(a, groups, shards, step_masks(gather_masks, count - 1)) for a in chains]
    gathered = []
    for low, high in zip(chains, highs):
        gathered += [low, high, swap(low, groups, shards, (1, 1)), swap(high, groups, shards, (1, 1))]
    total_rows = groups * rows
    gathered = [pltpu.with_memory_space_constraint(a, pltpu.VMEM) for a in gathered + [routes]]
    piece = (pairs, half_rows, 2 * width)

    def forward(*refs):
        forward_kernel(gather_masks, scatter_masks, groups, shards, experts, *refs)

    full, grads, keep, send = pl.pallas_call(
        forward,
        out_shape=(pltpu.VMEM((total_rows, features), BF), pltpu.VMEM((experts, total_rows, 2 * hidden), BF),
                   pltpu.VMEM(piece, F32), pltpu.VMEM(piece, BF)),
        in_specs=[VM] * 9 + [pl.BlockSpec(memory_space=pl.ANY)] * 3,
        out_specs=(VM,) * 4,
        scratch_shapes=[pltpu.VMEM((total_rows, features), BF), pltpu.VMEM((total_rows, features), BF),
                        pltpu.VMEM((experts, total_rows, 1), F32), pltpu.VMEM((total_rows, features), F32),
                        pltpu.VMEM(w_gate.shape, BF), pltpu.VMEM(w_up.shape, BF), pltpu.VMEM(w_down.shape, BF),
                        pltpu.SemaphoreType.DMA((3, experts))],
        compiler_params=pltpu.CompilerParams(vmem_limit_bytes=6 * experts * features * hidden + 16 * total_rows * features + 4 * MIB),
        cost_estimate=pl.CostEstimate(flops=10 * experts * total_rows * features * hidden, bytes_accessed=6 * experts * features * hidden, transcendentals=0),
        name="forward",
    )(*gathered, w_gate, w_up, w_down)

    blocks = 8
    shares = [3, 10, 8] + [5] * (count - 2)
    ends = [experts * blocks * sum(shares[:i + 1]) // sum(shares) for i in range(len(shares))]
    so_far, source, after = (), full, send
    kept = None
    for step in range(count + 1):
        units = list(range(ends[step - 1] if step else 0, ends[step]))
        grad_gate, grad_up, token, *made = weight_grads(source, grads, after, so_far, units, blocks, w_gate.shape, piece)
        so_far, source = (grad_gate, grad_up), made[0] if made else source
        if step == 0:
            kept = keep + swap(send, groups, shards, (1, 1)).astype(F32) + token
        else:
            half = kept.shape[0] // 2
            sent = kept[half:]
            if 2 * (step - 1) < count:
                sent = sent.astype(BF)
            kept = kept[:half] + swap(sent, groups, shards, step_masks(scatter_masks, step - 1)).astype(F32) + token
        after = kept
    done = kept[0].astype(BF)
    grad_tokens = jnp.concatenate([done[:, :width], done[:, width:]], 0)
    return grad_tokens, grad_gate, grad_up


def solution(mesh):
    in_specs = (
        P("group", "shard"),
        P("group", "shard"),
        P("group", None),
        P("group", None),
        P("group", None, "shard"),
        P("group", None, "shard"),
        P("group", "shard", None),
    )
    out_specs = (P("group", "shard"), P("group", None, "shard"), P("group", None, "shard"))
    return jax.shard_map(body, mesh=mesh, in_specs=in_specs, out_specs=out_specs, check_vma=False)
```

```python
import jax
import jax.numpy as jnp
from jax import lax
from jax.experimental import pallas as pl
from jax.experimental.pallas import tpu as pltpu
from jax.sharding import PartitionSpec as P

BF = jnp.bfloat16
F32 = jnp.float32
BOTH = ("group", "shard")
MIB = 1 << 20
VM = pl.BlockSpec(memory_space=pltpu.VMEM)
SM = pl.BlockSpec(memory_space=pltpu.SMEM)


def dot(a, b, da, db):
    return lax.dot_general(a, b, (((da,), (db,)), ((), ())), preferred_element_type=F32)


def bits_of(size):
    return size.bit_length() - 1


def stage_masks(groups, shards):
    masks = [1 << k for k in range(bits_of(shards) - 1, 0, -1)] + [shards << k for k in range(bits_of(groups))]
    other = masks[:-2] + masks[-2:][::-1]
    return other, masks


def swap(x, groups, shards, masks):
    pairs = [(i, i ^ masks[i & 1]) for i in range(groups * shards)]
    return lax.ppermute(x, BOTH, pairs)


def relative(index, masks, top_first):
    count = len(masks)
    out = 0
    for step, mask in enumerate(masks):
        place = count - 1 - step if top_first else step
        out = out | (((index >> bits_of(mask)) & 1) << place)
    return out


def load_kernel(experts, *refs):
    count = len(experts)
    sources, targets, token, sems = refs[:count], refs[count + 1:2 * count + 1], refs[-2], refs[-1]
    copies = [pltpu.make_async_copy(sources[k].at[experts[k]], targets[k], sems.at[k]) for k in range(count)]
    for copy in copies:
        copy.start()
    token[...] = jnp.zeros_like(token)
    for copy in copies:
        copy.wait()


def load(weights, items, after):
    experts = [e for _, e in items]
    chosen = [weights[i] for i, _ in items]

    def kernel(*refs):
        load_kernel(experts, *refs)

    *arrays, token = pl.pallas_call(
        kernel,
        out_shape=tuple(pltpu.VMEM(w.shape[1:], BF) for w in chosen) + (pltpu.VMEM((8, 128), F32),),
        in_specs=[pl.BlockSpec(memory_space=pl.ANY)] * len(items) + [VM],
        out_specs=(VM,) * (len(items) + 1),
        scratch_shapes=[pltpu.SemaphoreType.DMA((len(items),))],
        compiler_params=pltpu.CompilerParams(vmem_limit_bytes=MIB),
        cost_estimate=pl.CostEstimate(flops=0, bytes_accessed=sum(2 * w.size // w.shape[0] for w in chosen), transcendentals=0),
        name="load",
    )(*(pltpu.with_memory_space_constraint(w, pltpu.HBM) for w in chosen), pltpu.with_memory_space_constraint(after, pltpu.VMEM))
    return arrays, token


def forward_kernel(gather_masks, scatter_masks, groups, shards, experts, early,
                   t0, t1, t2, t3, c0, c1, c2, c3, routes, *refs):
    loaded, sources = refs[:early], refs[early:early + 3]
    full, grads, keep, send, qt, gt, *stores, sems = refs[-10:]
    half, rows, width = t0.shape[0], t0.shape[1], t0.shape[2] // 2
    tokens = 2 * groups * rows
    hidden = grads.shape[2] // 2
    group, shard = lax.axis_index("group"), lax.axis_index("shard")
    core, me = shard & 1, group * shards + shard
    gather_at = [relative(me, masks, False) for masks in gather_masks]
    scatter_at = [relative(me, masks, True) for masks in scatter_masks]

    order = [(i, e) for e in range(experts) for i in range(3)]
    late = order[early:]
    waiting = list(late)

    def fetch(i, e):
        return pltpu.make_async_copy(sources[i].at[e], stores[i].at[e - (experts - stores[i].shape[0])], sems.at[i, e])

    def release(number):
        for i, e in waiting[:number]:
            fetch(i, e).start()
        del waiting[:number]

    def weight(i, e):
        if (i, e) in late:
            return stores[i].at[e - (experts - stores[i].shape[0])]
        return loaded[order.index((i, e))]

    def arrived(i, e):
        if (i, e) in waiting:
            release(waiting.index((i, e)) + 1)
        if (i, e) in late:
            fetch(i, e).wait()

    release(4 if early else 3)

    def columns(own, other, g, pair):
        at = g * shards + pair * 2
        blocks = []
        for parity in range(2):
            r = relative(at, gather_masks[parity], False) ^ gather_at[parity]
            low, high = jnp.minimum(r, half - 1), jnp.maximum(r - half, 0)
            mine, theirs = (jnp.where(r < half, a[0][low], a[1][high]) for a in (own, other))
            blocks.append(jnp.where(core == parity, mine, theirs))
        return jnp.concatenate([jnp.concatenate([block[:, k * width:(k + 1) * width] for block in blocks], axis=1) for k in range(2)], axis=0)

    for g in range(groups):
        for pair in range(shards // 2):
            at = (slice(2 * g * rows, 2 * (g + 1) * rows), slice(2 * pair * width, 2 * (pair + 1) * width))
            full[at] = columns((t0, t1), (t2, t3), g, pair)
    for pair in range(shards // 2):
        block = jnp.concatenate([columns((c0, c1), (c2, c3), g, pair) for g in range(groups)], axis=0)
        qt[2 * pair * width:2 * (pair + 1) * width, :] = block.T

    tables = [routes[g ^ group].T for g in range(groups)]
    table = jnp.concatenate(tables, axis=0)
    def grads_of(e):
        number = (group * experts + e).astype(F32)
        coef = jnp.where(table[:, 0:1] == number, table[:, 2:3], 0.0) + jnp.where(table[:, 1:2] == number, table[:, 3:4], 0.0)
        arrived(0, e)
        gate_pre = dot(full[...], weight(0, e)[...], 1, 0)
        arrived(1, e)
        up_value = dot(full[...], weight(1, e)[...], 1, 0)
        arrived(2, e)
        hidden_grad = dot(weight(2, e)[...], qt[...], 1, 0).T * coef
        s = 1.0 / (1.0 + jnp.exp(-gate_pre))
        gate_grad = (hidden_grad * up_value * s * (1.0 + gate_pre * (1.0 - s))).astype(BF)
        up_grad = (hidden_grad * (gate_pre * s)).astype(BF)
        grads[e, :, :hidden] = gate_grad
        grads[e, :, hidden:] = up_grad
        gt[e, :hidden, :] = gate_grad.T
        gt[e, hidden:, :] = up_grad.T

    for e in range(experts):
        grads_of(e)
        release(3)
    for pair in range(shards // 2):
        at = slice(2 * pair * width, 2 * (pair + 1) * width)
        parts = [dot(weight(i, e)[at, :], gt[e, i * hidden:(i + 1) * hidden, :], 1, 0) for e in range(experts) for i in range(2)]
        total = sum(parts[1:], parts[0])
        total = total.T
        for g in range(groups):
            at = g * shards + pair * 2
            first = relative(at, scatter_masks[0], True) ^ scatter_at[0]
            second = relative(at, scatter_masks[1], True) ^ scatter_at[1]
            block = total[2 * g * rows:2 * (g + 1) * rows, :]
            even, odd = (jnp.concatenate([block[:rows, k * width:(k + 1) * width], block[rows:, k * width:(k + 1) * width]], axis=1) for k in range(2))
            keep[jnp.where(core == 0, first, second)] = jnp.where(core == 0, even, odd)
            send[jnp.where(core == 0, second, first)] = jnp.where(core == 0, odd, even).astype(BF)


def pack_kernel(tokens, cotangent, packed):
    half = tokens.shape[0] // 2
    for i, a in enumerate((tokens, cotangent)):
        packed[i, 0] = jnp.concatenate([a[:half, :], a[half:, :]], axis=1)


def route_kernel(ids, weights, after, routes):
    routes[0] = jnp.zeros_like(routes[0])
    routes[0, 0:2, :] = ids[...].astype(F32)
    routes[0, 2:4, :] = weights[...]


def pack(tokens, cotangent):
    rows, width = tokens.shape
    return pl.pallas_call(
        pack_kernel,
        out_shape=pltpu.VMEM((2, 1, rows // 2, 2 * width), BF),
        in_specs=[VM] * 2,
        out_specs=VM,
        name="pack",
    )(tokens, cotangent)


def pack_routes(ids, weights, after):
    return pl.pallas_call(
        route_kernel,
        out_shape=pltpu.VMEM((1, 8, ids.shape[0]), F32),
        in_specs=[VM] * 2 + [pl.BlockSpec(memory_space=pl.ANY)],
        out_specs=VM,
        name="pack_routes",
    )(ids.T, weights.T, after)


def weight_kernel(units, blocks, transposed, *refs):
    rows, grads = refs[0], refs[1]
    if transposed:
        out_gate, out_up, token, made, sems = refs[-5:]
        xt = rows
    else:
        out_gate, out_up, token, xt, made, sems = refs[-6:]
        xt[...] = rows[...].T
    features, hidden = xt.shape[0], out_gate.shape[2]
    block = features // blocks
    copies = []
    for k, unit in enumerate(units):
        expert, j = divmod(unit, blocks)
        at = slice(j * block, (j + 1) * block)
        for i, out in enumerate((out_gate, out_up)):
            made[i, k] = dot(xt[at, :], grads[expert, :, i * hidden:(i + 1) * hidden], 1, 0).astype(BF)
            copies.append(pltpu.make_async_copy(made.at[i, k], out.at[expert, at, :], sems.at[i, k]))
            copies[-1].start()
    token[...] = jnp.zeros_like(token)
    for copy in copies:
        copy.wait()


def weight_grads(rows, grads, after, so_far, units, blocks, shape, piece):
    experts, features, hidden = shape
    transposed = bool(so_far)
    array, zero = jax.ShapeDtypeStruct(shape, BF), pltpu.VMEM((1,) + piece[1:], F32)
    anywhere = pl.BlockSpec(memory_space=pl.ANY)

    def kernel(*refs):
        weight_kernel(units, blocks, transposed, *refs)

    return pl.pallas_call(
        kernel,
        out_shape=(array, array, zero) + (() if transposed else (pltpu.VMEM((features, rows.shape[0]), BF),)),
        in_specs=[VM] * 3 + [anywhere] * len(so_far),
        out_specs=(anywhere, anywhere, VM) + (() if transposed else (VM,)),
        input_output_aliases={3: 0, 4: 1} if transposed else {},
        scratch_shapes=[pltpu.VMEM((2, len(units), features // blocks, hidden), BF), pltpu.SemaphoreType.DMA((2, len(units)))],
        compiler_params=pltpu.CompilerParams(vmem_limit_bytes=16 * MIB),
        cost_estimate=pl.CostEstimate(flops=4 * features * grads.shape[1] * hidden, bytes_accessed=4 * features * hidden, transcendentals=0),
        name="weight_grads",
    )(*(pltpu.with_memory_space_constraint(a, pltpu.VMEM) for a in (rows, grads, after)), *so_far)


def body(tokens, cotangent, expert_ids, route_weight, w_gate, w_up, w_down):
    groups, shards = lax.axis_size("group"), lax.axis_size("shard")
    experts, features, hidden = w_gate.shape
    rows, width = tokens.shape
    half_rows = rows // 2
    gather_masks = stage_masks(groups, shards)
    scatter_masks = tuple(m[::-1] for m in gather_masks)
    count = len(gather_masks[0])
    pairs = groups * shards // 2

    def step_masks(masks, step):
        return masks[0][step], masks[1][step]

    packed = pack(tokens, cotangent)
    routes = pack_routes(expert_ids, route_weight, packed)
    def exchange(r):
        for k in range(bits_of(groups)):
            r = jnp.concatenate([r, swap(r, groups, shards, (shards << k,) * 2)], 0)
        return r

    routes = exchange(routes)
    weights = (w_gate, w_up, w_down)
    order = [(i, e) for e in range(experts) for i in range(3)]
    parts = (order[:2], order[2:6], order[6:9]) if experts > 3 else ((), (), ())
    early = sum(len(part) for part in parts)
    loaded, fences = [], []
    for step in range(count - 1):
        before, part = packed, parts[step - count + 3] if step > count - 4 else ()
        packed = jnp.concatenate([packed, swap(packed, groups, shards, step_masks(gather_masks, step))], 1)
        if part:
            arrays, token = load(weights, part, before)
            loaded += arrays
            packed, token = lax.optimization_barrier((packed, token))
            fences.append(token)
        if step == count - 3:
            packed, routes = lax.optimization_barrier((packed, routes))
    chains = [packed[0], packed[1]]
    highs = [swap(a, groups, shards, step_masks(gather_masks, count - 1)) for a in chains]
    others = [swap(a, groups, shards, (1, 1)) for a in chains]
    if parts[2]:
        arrays, token = load(weights, parts[2], others[1])
        loaded += arrays
        highs[0], token = lax.optimization_barrier((highs[0], token))
        fences.append(token)
    gathered = []
    for low, high, other in zip(chains, highs, others):
        gathered += [low, high, other, swap(high, groups, shards, (1, 1))]
    total_rows = groups * rows
    gathered = [pltpu.with_memory_space_constraint(a, pltpu.VMEM) for a in gathered + [routes]]
    piece = (pairs, half_rows, 2 * width)

    def forward(*refs):
        forward_kernel(gather_masks, scatter_masks, groups, shards, experts, early, *refs)

    loaded = [pltpu.with_memory_space_constraint(a, pltpu.VMEM) for a in loaded]
    full, grads, keep, send = pl.pallas_call(
        forward,
        out_shape=(pltpu.VMEM((total_rows, features), BF), pltpu.VMEM((experts, total_rows, 2 * hidden), BF),
                   pltpu.VMEM(piece, F32), pltpu.VMEM(piece, BF)),
        in_specs=[VM] * (9 + len(loaded)) + [pl.BlockSpec(memory_space=pl.ANY)] * (3 + len(fences)),
        out_specs=(VM,) * 4,
        scratch_shapes=[pltpu.VMEM((features, total_rows), BF), pltpu.VMEM((experts, 2 * hidden, total_rows), BF)]
        + [pltpu.VMEM((sum(j == i for j, _ in order[early:]),) + w.shape[1:], BF) for i, w in enumerate(weights)] + [pltpu.SemaphoreType.DMA((3, experts))],
        compiler_params=pltpu.CompilerParams(vmem_limit_bytes=2 * (3 * experts - early) * features * hidden + 20 * total_rows * features + 4 * MIB),
        cost_estimate=pl.CostEstimate(flops=10 * experts * total_rows * features * hidden, bytes_accessed=6 * experts * features * hidden, transcendentals=0),
        name="forward",
    )(*gathered, *loaded, *(pltpu.with_memory_space_constraint(w, pltpu.HBM) for w in weights), *fences)

    blocks = 8
    shares = [3, 10, 8] + [5] * (count - 2)
    ends = [experts * blocks * sum(shares[:i + 1]) // sum(shares) for i in range(len(shares))]
    so_far, source, after = (), full, send
    kept = None
    for step in range(count + 1):
        units = list(range(ends[step - 1] if step else 0, ends[step]))
        grad_gate, grad_up, token, *made = weight_grads(source, grads, after, so_far, units, blocks, w_gate.shape, piece)
        so_far, source = (grad_gate, grad_up), made[0] if made else source
        if step == 0:
            kept = keep + swap(send, groups, shards, (1, 1)).astype(F32) + token
        else:
            half = kept.shape[0] // 2
            sent = kept[half:]
            if 2 * (step - 1) < count:
                sent = sent.astype(BF)
            kept = kept[:half] + swap(sent, groups, shards, step_masks(scatter_masks, step - 1)).astype(F32) + token
        after = kept
    done = kept[0].astype(BF)
    grad_tokens = jnp.concatenate([done[:, :width], done[:, width:]], 0)
    return grad_tokens, grad_gate, grad_up


def solution(mesh):
    in_specs = (
        P("group", "shard"),
        P("group", "shard"),
        P("group", None),
        P("group", None),
        P("group", None, "shard"),
        P("group", None, "shard"),
        P("group", "shard", None),
    )
    out_specs = (P("group", "shard"), P("group", None, "shard"), P("group", None, "shard"))
    return jax.shard_map(body, mesh=mesh, in_specs=in_specs, out_specs=out_specs, check_vma=False)
```

```python
import jax
import jax.numpy as jnp
from jax import lax
from jax.experimental import pallas as pl
from jax.experimental.pallas import tpu as pltpu
from jax.sharding import PartitionSpec as P

BF = jnp.bfloat16
F32 = jnp.float32
BOTH = ("group", "shard")
MIB = 1 << 20
VM = pl.BlockSpec(memory_space=pltpu.VMEM)
SM = pl.BlockSpec(memory_space=pltpu.SMEM)


def dot(a, b, da, db):
    return lax.dot_general(a, b, (((da,), (db,)), ((), ())), preferred_element_type=F32)


def bits_of(size):
    return size.bit_length() - 1


def stage_masks(groups, shards):
    masks = [1 << k for k in range(bits_of(shards) - 1, 0, -1)] + [shards << k for k in range(bits_of(groups))]
    other = masks[:-2] + masks[-2:][::-1]
    return other, masks


def swap(x, groups, shards, masks):
    pairs = [(i, i ^ masks[i & 1]) for i in range(groups * shards)]
    return lax.ppermute(x, BOTH, pairs)


def relative(index, masks, top_first):
    count = len(masks)
    out = 0
    for step, mask in enumerate(masks):
        place = count - 1 - step if top_first else step
        out = out | (((index >> bits_of(mask)) & 1) << place)
    return out


def load_kernel(experts, *refs):
    count = len(experts)
    sources, targets, token, sems = refs[:count], refs[count + 1:2 * count + 1], refs[-2], refs[-1]
    copies = [pltpu.make_async_copy(sources[k].at[experts[k]], targets[k], sems.at[k]) for k in range(count)]
    for copy in copies:
        copy.start()
    token[...] = jnp.zeros_like(token)
    for copy in copies:
        copy.wait()


def load(weights, items, after):
    experts = [e for _, e in items]
    chosen = [weights[i] for i, _ in items]

    def kernel(*refs):
        load_kernel(experts, *refs)

    *arrays, token = pl.pallas_call(
        kernel,
        out_shape=tuple(pltpu.VMEM(w.shape[1:], BF) for w in chosen) + (pltpu.VMEM((8, 128), F32),),
        in_specs=[pl.BlockSpec(memory_space=pl.ANY)] * len(items) + [VM],
        out_specs=(VM,) * (len(items) + 1),
        scratch_shapes=[pltpu.SemaphoreType.DMA((len(items),))],
        compiler_params=pltpu.CompilerParams(vmem_limit_bytes=MIB),
        cost_estimate=pl.CostEstimate(flops=0, bytes_accessed=sum(2 * w.size // w.shape[0] for w in chosen), transcendentals=0),
        name="load",
    )(*(pltpu.with_memory_space_constraint(w, pltpu.HBM) for w in chosen), pltpu.with_memory_space_constraint(after, pltpu.VMEM))
    return arrays, token


def chip_columns(gather_masks, groups, shards, own, other, g, pair):
    half, width = own[0].shape[0], own[0].shape[2] // 2
    group, shard = lax.axis_index("group"), lax.axis_index("shard")
    core, me = shard & 1, group * shards + shard
    at = g * shards + pair * 2
    blocks = []
    for parity in range(2):
        r = relative(at, gather_masks[parity], False) ^ relative(me, gather_masks[parity], False)
        low, high = jnp.minimum(r, half - 1), jnp.maximum(r - half, 0)
        mine, theirs = (jnp.where(r < half, a[0][low], a[1][high]) for a in (own, other))
        blocks.append(jnp.where(core == parity, mine, theirs))
    return jnp.concatenate([jnp.concatenate([block[:, k * width:(k + 1) * width] for block in blocks], axis=1) for k in range(2)], axis=0)


def assemble_kernel(gather_masks, groups, shards, t0, t1, t2, t3, full):
    rows, width = t0.shape[1], t0.shape[2] // 2
    for g in range(groups):
        for pair in range(shards // 2):
            at = (slice(2 * g * rows, 2 * (g + 1) * rows), slice(2 * pair * width, 2 * (pair + 1) * width))
            full[at] = chip_columns(gather_masks, groups, shards, (t0, t1), (t2, t3), g, pair)


def assemble(gather_masks, groups, shards, parts, shape):
    def kernel(*refs):
        assemble_kernel(gather_masks, groups, shards, *refs)

    return pl.pallas_call(
        kernel,
        out_shape=pltpu.VMEM(shape, BF),
        in_specs=[VM] * 4,
        out_specs=VM,
        compiler_params=pltpu.CompilerParams(vmem_limit_bytes=8 * MIB),
        name="assemble",
    )(*parts)


def forward_kernel(gather_masks, scatter_masks, groups, shards, experts, early,
                   full, c0, c1, c2, c3, routes, *refs):
    loaded, sources = refs[:early], refs[early:early + 3]
    grads, keep, send, qt, gt, *stores, sems = refs[-9:]
    rows, width = c0.shape[1], c0.shape[2] // 2
    hidden = grads.shape[2] // 2
    group, shard = lax.axis_index("group"), lax.axis_index("shard")
    core, me = shard & 1, group * shards + shard
    scatter_at = [relative(me, masks, True) for masks in scatter_masks]

    order = [(i, e) for e in range(experts) for i in range(3)]
    late = order[early:]
    waiting = list(late)

    def fetch(i, e):
        return pltpu.make_async_copy(sources[i].at[e], stores[i].at[e - (experts - stores[i].shape[0])], sems.at[i, e])

    def release(number):
        for i, e in waiting[:number]:
            fetch(i, e).start()
        del waiting[:number]

    def weight(i, e):
        if (i, e) in late:
            return stores[i].at[e - (experts - stores[i].shape[0])]
        return loaded[order.index((i, e))]

    def arrived(i, e):
        if (i, e) in waiting:
            release(waiting.index((i, e)) + 1)
        if (i, e) in late:
            fetch(i, e).wait()

    release(4 if early else 3)

    for pair in range(shards // 2):
        block = jnp.concatenate([chip_columns(gather_masks, groups, shards, (c0, c1), (c2, c3), g, pair) for g in range(groups)], axis=0)
        qt[2 * pair * width:2 * (pair + 1) * width, :] = block.T

    tables = [routes[g ^ group].T for g in range(groups)]
    table = jnp.concatenate(tables, axis=0)
    def grads_of(e):
        number = (group * experts + e).astype(F32)
        coef = jnp.where(table[:, 0:1] == number, table[:, 2:3], 0.0) + jnp.where(table[:, 1:2] == number, table[:, 3:4], 0.0)
        arrived(0, e)
        gate_pre = dot(full[...], weight(0, e)[...], 1, 0)
        arrived(1, e)
        up_value = dot(full[...], weight(1, e)[...], 1, 0)
        arrived(2, e)
        hidden_grad = dot(weight(2, e)[...], qt[...], 1, 0).T * coef
        s = 1.0 / (1.0 + jnp.exp(-gate_pre))
        gate_grad = (hidden_grad * up_value * s * (1.0 + gate_pre * (1.0 - s))).astype(BF)
        up_grad = (hidden_grad * (gate_pre * s)).astype(BF)
        grads[e, :, :hidden] = gate_grad
        grads[e, :, hidden:] = up_grad
        gt[e, :hidden, :] = gate_grad.T
        gt[e, hidden:, :] = up_grad.T

    for e in range(experts):
        grads_of(e)
        release(3)
    for pair in range(shards // 2):
        at = slice(2 * pair * width, 2 * (pair + 1) * width)
        parts = [dot(weight(i, e)[at, :], gt[e, i * hidden:(i + 1) * hidden, :], 1, 0) for e in range(experts) for i in range(2)]
        total = sum(parts[1:], parts[0])
        total = total.T
        for g in range(groups):
            at = g * shards + pair * 2
            first = relative(at, scatter_masks[0], True) ^ scatter_at[0]
            second = relative(at, scatter_masks[1], True) ^ scatter_at[1]
            block = total[2 * g * rows:2 * (g + 1) * rows, :]
            even, odd = (jnp.concatenate([block[:rows, k * width:(k + 1) * width], block[rows:, k * width:(k + 1) * width]], axis=1) for k in range(2))
            keep[jnp.where(core == 0, first, second)] = jnp.where(core == 0, even, odd)
            send[jnp.where(core == 0, second, first)] = jnp.where(core == 0, odd, even).astype(BF)


def pack_kernel(tokens, cotangent, packed):
    half = tokens.shape[0] // 2
    for i, a in enumerate((tokens, cotangent)):
        packed[i, 0] = jnp.concatenate([a[:half, :], a[half:, :]], axis=1)


def route_kernel(ids, weights, after, routes):
    routes[0] = jnp.zeros_like(routes[0])
    routes[0, 0:2, :] = ids[...].astype(F32)
    routes[0, 2:4, :] = weights[...]


def pack(tokens, cotangent):
    rows, width = tokens.shape
    return pl.pallas_call(
        pack_kernel,
        out_shape=pltpu.VMEM((2, 1, rows // 2, 2 * width), BF),
        in_specs=[VM] * 2,
        out_specs=VM,
        name="pack",
    )(tokens, cotangent)


def pack_routes(ids, weights, after):
    return pl.pallas_call(
        route_kernel,
        out_shape=pltpu.VMEM((1, 8, ids.shape[0]), F32),
        in_specs=[VM] * 2 + [pl.BlockSpec(memory_space=pl.ANY)],
        out_specs=VM,
        name="pack_routes",
    )(ids.T, weights.T, after)


def weight_kernel(units, blocks, transposed, *refs):
    rows, grads = refs[0], refs[1]
    if transposed:
        out_gate, out_up, token, made, sems = refs[-5:]
        xt = rows
    else:
        out_gate, out_up, token, xt, made, sems = refs[-6:]
        xt[...] = rows[...].T
    features, hidden = xt.shape[0], out_gate.shape[2]
    block = features // blocks
    copies = []
    for k, unit in enumerate(units):
        expert, j = divmod(unit, blocks)
        at = slice(j * block, (j + 1) * block)
        for i, out in enumerate((out_gate, out_up)):
            made[i, k] = dot(xt[at, :], grads[expert, :, i * hidden:(i + 1) * hidden], 1, 0).astype(BF)
            copies.append(pltpu.make_async_copy(made.at[i, k], out.at[expert, at, :], sems.at[i, k]))
            copies[-1].start()
    token[...] = jnp.zeros_like(token)
    for copy in copies:
        copy.wait()


def weight_grads(rows, grads, after, so_far, units, blocks, shape, piece):
    experts, features, hidden = shape
    transposed = bool(so_far)
    array, zero = jax.ShapeDtypeStruct(shape, BF), pltpu.VMEM((1,) + piece[1:], F32)
    anywhere = pl.BlockSpec(memory_space=pl.ANY)

    def kernel(*refs):
        weight_kernel(units, blocks, transposed, *refs)

    return pl.pallas_call(
        kernel,
        out_shape=(array, array, zero) + (() if transposed else (pltpu.VMEM((features, rows.shape[0]), BF),)),
        in_specs=[VM] * 3 + [anywhere] * len(so_far),
        out_specs=(anywhere, anywhere, VM) + (() if transposed else (VM,)),
        input_output_aliases={3: 0, 4: 1} if transposed else {},
        scratch_shapes=[pltpu.VMEM((2, max(1, len(units)), features // blocks, hidden), BF), pltpu.SemaphoreType.DMA((2, max(1, len(units))))],
        compiler_params=pltpu.CompilerParams(vmem_limit_bytes=16 * MIB),
        cost_estimate=pl.CostEstimate(flops=4 * features * grads.shape[1] * hidden, bytes_accessed=4 * features * hidden, transcendentals=0),
        name="weight_grads",
    )(*(pltpu.with_memory_space_constraint(a, pltpu.VMEM) for a in (rows, grads, after)), *so_far)


def body(tokens, cotangent, expert_ids, route_weight, w_gate, w_up, w_down):
    groups, shards = lax.axis_size("group"), lax.axis_size("shard")
    experts, features, hidden = w_gate.shape
    rows, width = tokens.shape
    half_rows = rows // 2
    gather_masks = stage_masks(groups, shards)
    scatter_masks = tuple(m[::-1] for m in gather_masks)
    count = len(gather_masks[0])
    pairs = groups * shards // 2

    def step_masks(masks, step):
        return masks[0][step], masks[1][step]

    packed = pack(tokens, cotangent)
    routes = pack_routes(expert_ids, route_weight, packed)
    def exchange(r):
        for k in range(bits_of(groups)):
            r = jnp.concatenate([r, swap(r, groups, shards, (shards << k,) * 2)], 0)
        return r

    routes = exchange(routes)
    weights = (w_gate, w_up, w_down)
    order = [(i, e) for e in range(experts) for i in range(3)]
    parts = (order[:2], order[2:6], order[6:10]) if experts > 3 else ((), (), ())
    early = sum(len(part) for part in parts)
    loaded, fences = [], []
    for step in range(count - 1):
        before, part = packed, parts[step - count + 3] if step > count - 4 else ()
        packed = jnp.concatenate([packed, swap(packed, groups, shards, step_masks(gather_masks, step))], 1)
        if part:
            arrays, token = load(weights, part, before)
            loaded += arrays
            packed, token = lax.optimization_barrier((packed, token))
            fences.append(token)
        if step == count - 3:
            packed, routes = lax.optimization_barrier((packed, routes))
    chains = [packed[0], packed[1]]
    highs = [swap(a, groups, shards, step_masks(gather_masks, count - 1)) for a in chains]
    others = [swap(a, groups, shards, (1, 1)) for a in chains]
    if parts[2]:
        arrays, token = load(weights, parts[2], others[1])
        loaded += arrays
        highs[0], token = lax.optimization_barrier((highs[0], token))
        fences.append(token)
    gathered = []
    for low, high, other in zip(chains, highs, others):
        gathered += [low, high, other, swap(high, groups, shards, (1, 1))]
    total_rows = groups * rows
    gathered = [pltpu.with_memory_space_constraint(a, pltpu.VMEM) for a in gathered + [routes]]
    piece = (pairs, half_rows, 2 * width)

    def forward(*refs):
        forward_kernel(gather_masks, scatter_masks, groups, shards, experts, early, *refs)

    loaded = [pltpu.with_memory_space_constraint(a, pltpu.VMEM) for a in loaded]
    full = assemble(gather_masks, groups, shards, gathered[:4], (total_rows, features))
    grads, keep, send = pl.pallas_call(
        forward,
        out_shape=(pltpu.VMEM((experts, total_rows, 2 * hidden), BF),
                   pltpu.VMEM(piece, F32), pltpu.VMEM(piece, BF)),
        in_specs=[VM] * (6 + len(loaded)) + [pl.BlockSpec(memory_space=pl.ANY)] * (3 + len(fences)),
        out_specs=(VM,) * 3,
        scratch_shapes=[pltpu.VMEM((features, total_rows), BF), pltpu.VMEM((experts, 2 * hidden, total_rows), BF)]
        + [pltpu.VMEM((sum(j == i for j, _ in order[early:]),) + w.shape[1:], BF) for i, w in enumerate(weights)] + [pltpu.SemaphoreType.DMA((3, experts))],
        compiler_params=pltpu.CompilerParams(vmem_limit_bytes=2 * (3 * experts - early) * features * hidden + 20 * total_rows * features + 4 * MIB),
        cost_estimate=pl.CostEstimate(flops=10 * experts * total_rows * features * hidden, bytes_accessed=6 * experts * features * hidden, transcendentals=0),
        name="forward",
    )(pltpu.with_memory_space_constraint(full, pltpu.VMEM), *gathered[4:], *loaded, *(pltpu.with_memory_space_constraint(w, pltpu.HBM) for w in weights), *fences)

    blocks = 8
    shares = [3, 11, 9, 6] + [3] * (count - 3)
    ends = [experts * blocks * sum(shares[:i + 1]) // sum(shares) for i in range(len(shares))]
    so_far, source, after = (), full, send
    kept = None
    for step in range(count + 1):
        units = list(range(ends[step - 1] if step else 0, ends[step]))
        grad_gate, grad_up, token, *made = weight_grads(source, grads, after, so_far, units, blocks, w_gate.shape, piece)
        so_far, source = (grad_gate, grad_up), made[0] if made else source
        if step == 0:
            kept = keep + swap(send, groups, shards, (1, 1)).astype(F32) + token
        else:
            half = kept.shape[0] // 2
            sent = kept[half:]
            if 2 * (step - 1) < count:
                sent = sent.astype(BF)
            kept = kept[:half] + swap(sent, groups, shards, step_masks(scatter_masks, step - 1)).astype(F32) + token
        after = kept
    done = kept[0].astype(BF)
    grad_tokens = jnp.concatenate([done[:, :width], done[:, width:]], 0)
    return grad_tokens, grad_gate, grad_up


def solution(mesh):
    in_specs = (
        P("group", "shard"),
        P("group", "shard"),
        P("group", None),
        P("group", None),
        P("group", None, "shard"),
        P("group", None, "shard"),
        P("group", "shard", None),
    )
    out_specs = (P("group", "shard"), P("group", None, "shard"), P("group", None, "shard"))
    return jax.shard_map(body, mesh=mesh, in_specs=in_specs, out_specs=out_specs, check_vma=False)
```

```python
import jax
import jax.numpy as jnp
from jax import lax
from jax.experimental import pallas as pl
from jax.experimental.pallas import tpu as pltpu
from jax.sharding import PartitionSpec as P

BF = jnp.bfloat16
F32 = jnp.float32
BOTH = ("group", "shard")
MIB = 1 << 20
VM = pl.BlockSpec(memory_space=pltpu.VMEM)
SM = pl.BlockSpec(memory_space=pltpu.SMEM)


def dot(a, b, da, db):
    return lax.dot_general(a, b, (((da,), (db,)), ((), ())), preferred_element_type=F32)


def bits_of(size):
    return size.bit_length() - 1


def stage_masks(groups, shards):
    masks = [1 << k for k in range(bits_of(shards) - 1, 0, -1)] + [shards << k for k in range(bits_of(groups))]
    other = masks[:-2] + masks[-2:][::-1]
    return other, masks


def swap(x, groups, shards, masks):
    pairs = [(i, i ^ masks[i & 1]) for i in range(groups * shards)]
    return lax.ppermute(x, BOTH, pairs)


def relative(index, masks, top_first):
    count = len(masks)
    out = 0
    for step, mask in enumerate(masks):
        place = count - 1 - step if top_first else step
        out = out | (((index >> bits_of(mask)) & 1) << place)
    return out


def load_kernel(experts, *refs):
    count = len(experts)
    sources, targets, token, sems = refs[:count], refs[count + 1:2 * count + 1], refs[-2], refs[-1]
    copies = [pltpu.make_async_copy(sources[k].at[experts[k]], targets[k], sems.at[k]) for k in range(count)]
    for copy in copies:
        copy.start()
    token[...] = jnp.zeros_like(token)
    for copy in copies:
        copy.wait()


def load(weights, items, after):
    experts = [e for _, e in items]
    chosen = [weights[i] for i, _ in items]

    def kernel(*refs):
        load_kernel(experts, *refs)

    *arrays, token = pl.pallas_call(
        kernel,
        out_shape=tuple(pltpu.VMEM(w.shape[1:], BF) for w in chosen) + (pltpu.VMEM((8, 128), F32),),
        in_specs=[pl.BlockSpec(memory_space=pl.ANY)] * len(items) + [VM],
        out_specs=(VM,) * (len(items) + 1),
        scratch_shapes=[pltpu.SemaphoreType.DMA((len(items),))],
        compiler_params=pltpu.CompilerParams(vmem_limit_bytes=MIB),
        cost_estimate=pl.CostEstimate(flops=0, bytes_accessed=sum(2 * w.size // w.shape[0] for w in chosen), transcendentals=0),
        name="load",
    )(*(pltpu.with_memory_space_constraint(w, pltpu.HBM) for w in chosen), pltpu.with_memory_space_constraint(after, pltpu.VMEM))
    return arrays, token


def chip_columns(gather_masks, groups, shards, own, other, g, pair):
    half, width = own[0].shape[0], own[0].shape[2] // 2
    group, shard = lax.axis_index("group"), lax.axis_index("shard")
    core, me = shard & 1, group * shards + shard
    at = g * shards + pair * 2
    blocks = []
    for parity in range(2):
        r = relative(at, gather_masks[parity], False) ^ relative(me, gather_masks[parity], False)
        low, high = jnp.minimum(r, half - 1), jnp.maximum(r - half, 0)
        mine, theirs = (jnp.where(r < half, a[0][low], a[1][high]) for a in (own, other))
        blocks.append(jnp.where(core == parity, mine, theirs))
    return jnp.concatenate([jnp.concatenate([block[:, k * width:(k + 1) * width] for block in blocks], axis=1) for k in range(2)], axis=0)


def assemble_kernel(gather_masks, groups, shards, t0, t1, t2, t3, full, xt):
    rows, width = t0.shape[1], t0.shape[2] // 2
    for g in range(groups):
        for pair in range(shards // 2):
            at = (slice(2 * g * rows, 2 * (g + 1) * rows), slice(2 * pair * width, 2 * (pair + 1) * width))
            full[at] = chip_columns(gather_masks, groups, shards, (t0, t1), (t2, t3), g, pair)
    xt[...] = full[...].T


def assemble(gather_masks, groups, shards, parts, shape):
    def kernel(*refs):
        assemble_kernel(gather_masks, groups, shards, *refs)

    return pl.pallas_call(
        kernel,
        out_shape=(pltpu.VMEM(shape, BF), pltpu.VMEM(shape[::-1], BF)),
        in_specs=[VM] * 4,
        out_specs=(VM, VM),
        compiler_params=pltpu.CompilerParams(vmem_limit_bytes=8 * MIB),
        name="assemble",
    )(*parts)


def forward_kernel(gather_masks, scatter_masks, groups, shards, experts, early,
                   full, c0, c1, c2, c3, routes, *refs):
    loaded, sources = refs[:early], refs[early:early + 3]
    grads, keep, send, qt, gt, *stores, sems = refs[-9:]
    rows, width = c0.shape[1], c0.shape[2] // 2
    hidden = grads.shape[2] // 2
    group, shard = lax.axis_index("group"), lax.axis_index("shard")
    core, me = shard & 1, group * shards + shard
    scatter_at = [relative(me, masks, True) for masks in scatter_masks]

    order = [(i, e) for e in range(experts) for i in range(3)]
    late = order[early:]
    waiting = list(late)

    def fetch(i, e):
        return pltpu.make_async_copy(sources[i].at[e], stores[i].at[e - (experts - stores[i].shape[0])], sems.at[i, e])

    def release(number):
        for i, e in waiting[:number]:
            fetch(i, e).start()
        del waiting[:number]

    def weight(i, e):
        if (i, e) in late:
            return stores[i].at[e - (experts - stores[i].shape[0])]
        return loaded[order.index((i, e))]

    def arrived(i, e):
        if (i, e) in waiting:
            release(waiting.index((i, e)) + 1)
        if (i, e) in late:
            fetch(i, e).wait()

    release(4 if early else 3)

    for pair in range(shards // 2):
        block = jnp.concatenate([chip_columns(gather_masks, groups, shards, (c0, c1), (c2, c3), g, pair) for g in range(groups)], axis=0)
        qt[2 * pair * width:2 * (pair + 1) * width, :] = block.T

    tables = [routes[g ^ group].T for g in range(groups)]
    table = jnp.concatenate(tables, axis=0)
    def grads_of(e):
        number = (group * experts + e).astype(F32)
        coef = jnp.where(table[:, 0:1] == number, table[:, 2:3], 0.0) + jnp.where(table[:, 1:2] == number, table[:, 3:4], 0.0)
        arrived(0, e)
        gate_pre = dot(full[...], weight(0, e)[...], 1, 0)
        arrived(1, e)
        up_value = dot(full[...], weight(1, e)[...], 1, 0)
        arrived(2, e)
        hidden_grad = dot(weight(2, e)[...], qt[...], 1, 0).T * coef
        s = 1.0 / (1.0 + jnp.exp(-gate_pre))
        gate_grad = (hidden_grad * up_value * s * (1.0 + gate_pre * (1.0 - s))).astype(BF)
        up_grad = (hidden_grad * (gate_pre * s)).astype(BF)
        grads[e, :, :hidden] = gate_grad
        grads[e, :, hidden:] = up_grad
        gt[e, :hidden, :] = gate_grad.T
        gt[e, hidden:, :] = up_grad.T

    for e in range(experts):
        grads_of(e)
        release(3)
    for pair in range(shards // 2):
        at = slice(2 * pair * width, 2 * (pair + 1) * width)
        parts = [dot(weight(i, e)[at, :], gt[e, i * hidden:(i + 1) * hidden, :], 1, 0) for e in range(experts) for i in range(2)]
        total = sum(parts[1:], parts[0])
        total = total.T
        for g in range(groups):
            at = g * shards + pair * 2
            first = relative(at, scatter_masks[0], True) ^ scatter_at[0]
            second = relative(at, scatter_masks[1], True) ^ scatter_at[1]
            block = total[2 * g * rows:2 * (g + 1) * rows, :]
            even, odd = (jnp.concatenate([block[:rows, k * width:(k + 1) * width], block[rows:, k * width:(k + 1) * width]], axis=1) for k in range(2))
            keep[jnp.where(core == 0, first, second)] = jnp.where(core == 0, even, odd)
            send[jnp.where(core == 0, second, first)] = jnp.where(core == 0, odd, even).astype(BF)


def pack_kernel(tokens, cotangent, packed):
    half = tokens.shape[0] // 2
    for i, a in enumerate((tokens, cotangent)):
        packed[i, 0] = jnp.concatenate([a[:half, :], a[half:, :]], axis=1)


def route_kernel(ids, weights, after, routes):
    routes[0] = jnp.zeros_like(routes[0])
    routes[0, 0:2, :] = ids[...].astype(F32)
    routes[0, 2:4, :] = weights[...]


def pack(tokens, cotangent):
    rows, width = tokens.shape
    return pl.pallas_call(
        pack_kernel,
        out_shape=pltpu.VMEM((2, 1, rows // 2, 2 * width), BF),
        in_specs=[VM] * 2,
        out_specs=VM,
        name="pack",
    )(tokens, cotangent)


def pack_routes(ids, weights, after):
    return pl.pallas_call(
        route_kernel,
        out_shape=pltpu.VMEM((1, 8, ids.shape[0]), F32),
        in_specs=[VM] * 2 + [pl.BlockSpec(memory_space=pl.ANY)],
        out_specs=VM,
        name="pack_routes",
    )(ids.T, weights.T, after)


def weight_kernel(units, blocks, xt, grads, *refs):
    out_gate, out_up, token, made, sems = refs[-5:]
    features, hidden = xt.shape[0], out_gate.shape[2]
    block = features // blocks
    copies = []
    for k, unit in enumerate(units):
        expert, j = divmod(unit, blocks)
        at = slice(j * block, (j + 1) * block)
        for i, out in enumerate((out_gate, out_up)):
            made[i, k] = dot(xt[at, :], grads[expert, :, i * hidden:(i + 1) * hidden], 1, 0).astype(BF)
            copies.append(pltpu.make_async_copy(made.at[i, k], out.at[expert, at, :], sems.at[i, k]))
            copies[-1].start()
    token[...] = jnp.zeros_like(token)
    for copy in copies:
        copy.wait()


def weight_grads(rows, grads, after, so_far, units, blocks, shape, piece):
    experts, features, hidden = shape
    array, zero = jax.ShapeDtypeStruct(shape, BF), pltpu.VMEM((1,) + piece[1:], F32)
    anywhere = pl.BlockSpec(memory_space=pl.ANY)

    def kernel(*refs):
        weight_kernel(units, blocks, *refs)

    return pl.pallas_call(
        kernel,
        out_shape=(array, array, zero),
        in_specs=[VM] * 3 + [anywhere] * len(so_far),
        out_specs=(anywhere, anywhere, VM),
        input_output_aliases={3: 0, 4: 1} if so_far else {},
        scratch_shapes=[pltpu.VMEM((2, max(1, len(units)), features // blocks, hidden), BF), pltpu.SemaphoreType.DMA((2, max(1, len(units))))],
        compiler_params=pltpu.CompilerParams(vmem_limit_bytes=16 * MIB),
        cost_estimate=pl.CostEstimate(flops=4 * features * grads.shape[1] * hidden, bytes_accessed=4 * features * hidden, transcendentals=0),
        name="weight_grads",
    )(*(pltpu.with_memory_space_constraint(a, pltpu.VMEM) for a in (rows, grads, after)), *so_far)


def body(tokens, cotangent, expert_ids, route_weight, w_gate, w_up, w_down):
    groups, shards = lax.axis_size("group"), lax.axis_size("shard")
    experts, features, hidden = w_gate.shape
    rows, width = tokens.shape
    half_rows = rows // 2
    gather_masks = stage_masks(groups, shards)
    scatter_masks = tuple(m[::-1] for m in gather_masks)
    count = len(gather_masks[0])
    pairs = groups * shards // 2

    def step_masks(masks, step):
        return masks[0][step], masks[1][step]

    packed = pack(tokens, cotangent)
    routes = pack_routes(expert_ids, route_weight, packed)
    def exchange(r):
        for k in range(bits_of(groups)):
            r = jnp.concatenate([r, swap(r, groups, shards, (shards << k,) * 2)], 0)
        return r

    routes = exchange(routes)
    weights = (w_gate, w_up, w_down)
    order = [(i, e) for e in range(experts) for i in range(3)]
    parts = (order[:2], order[2:6], order[6:10]) if experts > 3 else ((), (), ())
    early = sum(len(part) for part in parts)
    loaded, fences = [], []
    for step in range(count - 1):
        before, part = packed, parts[step - count + 3] if step > count - 4 else ()
        packed = jnp.concatenate([packed, swap(packed, groups, shards, step_masks(gather_masks, step))], 1)
        if part:
            arrays, token = load(weights, part, before)
            loaded += arrays
            packed, token = lax.optimization_barrier((packed, token))
            fences.append(token)
        if step == count - 3:
            packed, routes = lax.optimization_barrier((packed, routes))
    chains = [packed[0], packed[1]]
    highs = [swap(a, groups, shards, step_masks(gather_masks, count - 1)) for a in chains]
    others = [swap(a, groups, shards, (1, 1)) for a in chains]
    if parts[2]:
        arrays, token = load(weights, parts[2], others[1])
        loaded += arrays
        highs[0], token = lax.optimization_barrier((highs[0], token))
        fences.append(token)
    gathered = []
    for low, high, other in zip(chains, highs, others):
        gathered += [low, high, other, swap(high, groups, shards, (1, 1))]
    total_rows = groups * rows
    gathered = [pltpu.with_memory_space_constraint(a, pltpu.VMEM) for a in gathered + [routes]]
    piece = (pairs, half_rows, 2 * width)

    def forward(*refs):
        forward_kernel(gather_masks, scatter_masks, groups, shards, experts, early, *refs)

    loaded = [pltpu.with_memory_space_constraint(a, pltpu.VMEM) for a in loaded]
    full, xt = assemble(gather_masks, groups, shards, gathered[:4], (total_rows, features))
    grads, keep, send = pl.pallas_call(
        forward,
        out_shape=(pltpu.VMEM((experts, total_rows, 2 * hidden), BF),
                   pltpu.VMEM(piece, F32), pltpu.VMEM(piece, BF)),
        in_specs=[VM] * (6 + len(loaded)) + [pl.BlockSpec(memory_space=pl.ANY)] * (3 + len(fences)),
        out_specs=(VM,) * 3,
        scratch_shapes=[pltpu.VMEM((features, total_rows), BF), pltpu.VMEM((experts, 2 * hidden, total_rows), BF)]
        + [pltpu.VMEM((sum(j == i for j, _ in order[early:]),) + w.shape[1:], BF) for i, w in enumerate(weights)] + [pltpu.SemaphoreType.DMA((3, experts))],
        compiler_params=pltpu.CompilerParams(vmem_limit_bytes=2 * (3 * experts - early) * features * hidden + 20 * total_rows * features + 4 * MIB),
        cost_estimate=pl.CostEstimate(flops=10 * experts * total_rows * features * hidden, bytes_accessed=6 * experts * features * hidden, transcendentals=0),
        name="forward",
    )(pltpu.with_memory_space_constraint(full, pltpu.VMEM), *gathered[4:], *loaded, *(pltpu.with_memory_space_constraint(w, pltpu.HBM) for w in weights), *fences)

    blocks = 8
    shares = [3, 11, 9, 6] + [3] * (count - 3)
    ends = [experts * blocks * sum(shares[:i + 1]) // sum(shares) for i in range(len(shares))]
    so_far, after = (), send
    kept = None
    for step in range(count + 1):
        units = list(range(ends[step - 1] if step else 0, ends[step]))
        grad_gate, grad_up, token = weight_grads(xt, grads, after, so_far, units, blocks, w_gate.shape, piece)
        so_far = (grad_gate, grad_up)
        if step == 0:
            kept = keep + swap(send, groups, shards, (1, 1)).astype(F32) + token
        else:
            half = kept.shape[0] // 2
            sent = kept[half:]
            if step < count:
                sent = sent.astype(BF)
            kept = kept[:half] + swap(sent, groups, shards, step_masks(scatter_masks, step - 1)).astype(F32) + token
        after = kept
    done = kept[0].astype(BF)
    grad_tokens = jnp.concatenate([done[:, :width], done[:, width:]], 0)
    return grad_tokens, grad_gate, grad_up


def solution(mesh):
    in_specs = (
        P("group", "shard"),
        P("group", "shard"),
        P("group", None),
        P("group", None),
        P("group", None, "shard"),
        P("group", None, "shard"),
        P("group", "shard", None),
    )
    out_specs = (P("group", "shard"), P("group", None, "shard"), P("group", None, "shard"))
    return jax.shard_map(body, mesh=mesh, in_specs=in_specs, out_specs=out_specs, check_vma=False)
```
